32 devices in a mesh: groups: 2 (over x), train: 8 (over z, y), test: 2 (over core).
Axes of the slice: x: 2, y: 2, z: 4, core: 2. Of those that a mesh axis runs over, the one named last changes fastest.
Arguments:
- train_grads: bfloat16 [16384, 8192], P(('groups', 'train'), 'test'), parts along dimension 0, may hold values from -0.0625 to 0.0625
- test_grads: float32 [256, 8192], P('test', 'train'), may hold values from -6 to 6
- fisher_inverse: float32 [8192, 8192], P('train', 'test'), may hold values from -1 to 2.5
Outputs:
- scores: float32 [16384, 256], P(('groups', 'train'), 'test'), parts along dimension 0
The draws below stay inside these ranges and needn't reach their ends.
There are 2 independent parts, one for each index of `groups`. The reference program is written for one: setup_inputs(seed, part) draws one part's arguments, and reference() takes and returns one part's arrays. A program takes and returns all parts, laid end to end along the dimension named above; an argument that names none is the same for every part. Nothing has to cross between parts.
All inputs are finite; a program needn't handle non-finite values.
Results may differ from the reference program's by a relative error of at most 0.0029.
Values may be sent and summed in bfloat16 or wider, within the bound.
A program may use at most 128 MiB of HBM per device.

```python
import jax
import jax.numpy as jnp
from jax import lax

K = 8192
QUERIES = 256
TRAIN_DEV = 1024
TRAIN = 8192


def draw_fisher_inverse(key, part):
    key = jax.random.fold_in(key, 11)
    key_off = jax.random.fold_in(key, 1)
    key_diag = jax.random.fold_in(key, 2)
    spread = 0.2 / K ** 0.5
    base = jax.random.normal(key_off, (K, K), jnp.float32) * spread
    symmetric = (base + base.T) * 0.7071
    diagonal = jnp.exp(jax.random.uniform(key_diag, (K,), jnp.float32, jnp.log(0.5), jnp.log(2.0)))
    rows = lax.broadcasted_iota(jnp.int32, (K, K), 0)
    columns = lax.broadcasted_iota(jnp.int32, (K, K), 1)
    return jnp.where(rows == columns, diagonal[:, None], symmetric)


def with_spikes(array, stream_key, source, target, parts, factor):
    owner, partner = [(jnp.arange(array.shape[dim]) // (array.shape[dim] // parts)).reshape([-1 if axis == dim else 1 for axis in range(array.ndim)]) for dim in (source, target)]
    chosen = jax.random.permutation(stream_key, parts)[partner]
    strong = (owner == chosen) | (owner == (partner + parts // 2) % parts)
    return jnp.where(strong, factor * array, array)


def levels(key, extent, cuts, smallest, largest):
    def one(position, parts):
        draws = jax.random.uniform(jax.random.fold_in(jax.random.fold_in(key, 6), position), (parts,), jnp.float32, smallest / len(cuts), largest / len(cuts))
        return jnp.repeat(jnp.exp(draws), extent[position] // parts).reshape((-1,) + (1,) * (len(extent) - position - 1))

    loudness = one(*cuts[0])
    for cut in cuts[1:]:
        loudness = loudness * one(*cut)
    return loudness


def bell_draw(stream_key, dims, scale, limit, pieces=(), kind=jnp.bfloat16):
    result = scale * jax.random.normal(stream_key, dims, jnp.float32)
    if pieces:
        result = result * levels(stream_key, dims, pieces, -0.22, 0.18)
    return jnp.clip(result, -limit, limit).astype(kind)


def bell_draw_with(rng, extent, width, reach, split, heavy, held_as=jnp.bfloat16):
    entries = width * jax.random.normal(rng, extent, jnp.float32)
    if split:
        entries = entries * levels(rng, extent, split, -0.22, 0.18)
    return jnp.clip(with_spikes(entries, jax.random.fold_in(rng, 3), *heavy), -reach, reach).astype(held_as)


def setup_inputs(seed: int = 0, part: int = 0) -> dict:
    arg_keys = jax.random.split(jax.random.key(seed), 4)
    part_splits = jax.random.split(jax.random.fold_in(arg_keys[3], part), 4)
    train_grads = bell_draw(part_splits[0], (TRAIN, K), K ** -0.5, 0.0625, ((0, 8), (1, 2)))
    test_grads = bell_draw_with(arg_keys[1], (QUERIES, K), 1.0, 6.0, ((0, 2), (1, 8)), (1, 0, 8, 2.0), jnp.float32)
    fisher_inverse = draw_fisher_inverse(jax.random.fold_in(arg_keys[3], 71), part)
    return {"train_grads": train_grads, "test_grads": test_grads, "fisher_inverse": fisher_inverse}


def reference(train_grads, test_grads, fisher_inverse):
    preconditioned = jnp.dot(test_grads, fisher_inverse, precision=lax.Precision.HIGHEST, preferred_element_type=jnp.float32).astype(jnp.bfloat16)
    right_side = preconditioned.astype(jnp.float32)
    blocks = train_grads.reshape(TRAIN // TRAIN_DEV, TRAIN_DEV, K)

    def score_block(block):
        return jnp.dot(block.astype(jnp.float32), right_side.T, precision=lax.Precision.HIGHEST, preferred_element_type=jnp.float32)

    scores = lax.map(score_block, blocks)
    return scores.reshape(TRAIN, QUERIES)
```

```python
import jax
import jax.numpy as jnp
from jax import lax
from jax.experimental import pallas as pl
from jax.experimental.pallas import tpu as pltpu
from jax.sharding import PartitionSpec as P

MESH = pl.DeviceIdType.MESH
F32 = jnp.float32
BF16 = jnp.bfloat16

NY = 2
NZ = 4
CHUNKS = 8
SEND_Y = BF16
SEND_Z = BF16


def tile_scores(train_grads, pieces):
    return lax.dot_general(
        train_grads, pieces, (((1,), (1,)), ((), ())), preferred_element_type=F32
    )


def kernel(
    train_ref, test_ref, fisher_ref, out_ref,
    f_buf, g_buf, t_buf, lhs, part_nb, recv_y, part_own, zsend, zrecv, pre,
    acc_far, acc_own, recv_sc,
    f_sem, g_sem, t_sem, ts_sem, tr_sem, ys, yr, zs, zr, gs, gr, cs, cr, xs, xr, ss, sr,
):
    queries, depth = t_buf.shape
    half_q = queries // 2
    width = f_buf.shape[1]
    quarter = width // 2
    tile = quarter // NZ
    rows = queries // CHUNKS
    pair = 2 * tile
    stride = quarter * NY

    g = lax.axis_index("groups")
    t = lax.axis_index("train")
    c = lax.axis_index("test")
    z = t // NY
    y = t % NY
    core = (g, t, 1 - c)
    side = (g, z * NY + 1 - y, c)
    twin = (1 - g, t, c)

    def peer(d):
        return (g, lax.rem(z + d, NZ) * NY + y, c)

    def column(who_g, who_y, piece):
        return piece * stride + who_y * quarter + who_g * pair

    def f_copy(i):
        who = jnp.where(i < NZ, 1 - y, y) if not isinstance(i, int) else (1 - y if i < NZ else y)
        k = i % NZ
        start = column(g, who, k // 2) + (k % 2) * tile
        return pltpu.make_async_copy(
            fisher_ref.at[:, pl.ds(pl.multiple_of(start, tile), tile)],
            f_buf.at[:, pl.ds(pl.multiple_of(i * tile, tile), tile)],
            f_sem.at[i],
        )

    def g_copy(i):
        who_g, who_y, piece = i // 4, (i // 2) % 2, i % 2
        return pltpu.make_async_copy(
            train_ref.at[:, pl.ds(column(who_g, who_y, piece), pair)],
            g_buf.at[:, pl.ds(i * pair, pair)],
            g_sem.at[i],
        )

    mine = pl.ds(pl.multiple_of(c * half_q, half_q), half_q)
    t_copy = pltpu.make_async_copy(test_ref, t_buf.at[mine], t_sem)
    t_copy.start()
    for i in range(2 * NZ):
        f_copy(i).start()

    barrier = pltpu.get_barrier_semaphore()
    friends = [core, side, twin] + [peer(d) for d in range(1, NZ)]
    for friend in friends:
        pl.semaphore_signal(barrier, inc=1, device_id=friend, device_id_type=MESH)
    pl.semaphore_wait(barrier, len(friends))

    def remote(src, dst, send, recv, where):
        return pltpu.make_async_remote_copy(
            src_ref=src, dst_ref=dst, send_sem=send, recv_sem=recv,
            device_id=where, device_id_type=MESH,
        )

    t_send = remote(test_ref, t_buf.at[mine], ts_sem, tr_sem, core)
    t_send.start()
    for i in range(8):
        g_copy(i).start()
    t_copy.wait()
    t_send.wait_recv()
    values = t_buf[...]
    high = values.astype(BF16)
    lhs[:queries, :] = high
    lhs[queries:, :] = (values - high.astype(F32)).astype(BF16)

    def product(i):
        f_copy(i).wait()
        f = f_buf[:, pl.ds(pl.multiple_of(i * tile, tile), tile)]
        f_high = f.astype(BF16)
        f_low = (f - f_high.astype(F32)).astype(BF16)
        both = jnp.dot(lhs[...], f_high, preferred_element_type=F32)
        cross = jnp.dot(lhs[:queries, :], f_low, preferred_element_type=F32)
        return both[:queries] + (both[queries:] + cross)

    @pl.loop(0, NZ)
    def _(i):
        part_nb[:, pl.ds(pl.multiple_of(i * tile, tile), tile)] = product(i).astype(SEND_Y)

    def chunk(j):
        n = CHUNKS // 2
        start = (1 - c) * half_q + j * rows if j < n else c * half_q + (j - n) * rows
        return pl.ds(pl.multiple_of(start, rows), rows)

    def y_sum(j):
        return remote(part_nb.at[chunk(j)], recv_y.at[chunk(j)], ys.at[j], yr.at[j], side)

    for j in range(CHUNKS):
        y_sum(j).start()

    @pl.loop(NZ, 2 * NZ)
    def _(i):
        part_own[:, pl.ds(pl.multiple_of((i - NZ) * tile, tile), tile)] = product(i)

    def tile_of(d):
        k = lax.rem(z + d + NZ - 2 * c, NZ)
        return (k % 2) * 2 + k // 2

    def tile_cols(d, base=0):
        return pl.ds(pl.multiple_of(base + tile_of(d) * tile, tile), tile)

    def share(who_g, who_y):
        start = who_g * width + who_y * quarter
        return pl.ds(pl.multiple_of(start, quarter), quarter)

    def z_sum(j, d):
        return remote(
            zsend.at[chunk(j), tile_cols(d)], zrecv.at[d - 1, chunk(j)],
            zs.at[j, d - 1], zr.at[j, d - 1], peer(d),
        )

    def z_gather(j, d):
        place = pre.at[chunk(j), tile_cols(0, g * width + y * quarter)]
        return remote(place, place, gs.at[j, d - 1], gr.at[j, d - 1], peer(d))

    def y_gather(j):
        place = pre.at[chunk(j), share(g, y)]
        return remote(place, place, cs.at[j], cr.at[j], side)

    def x_gather(j, which):
        place = pre.at[chunk(j), share(g, y if which == 0 else 1 - y)]
        return remote(place, place, xs.at[j, which], xr.at[j, which], twin)

    def stage_a(j):
        y_sum(j).wait_recv()
        total = part_own[chunk(j), :] + recv_y[chunk(j), :].astype(F32)
        part_own[chunk(j), :] = total
        zsend[chunk(j), :] = total.astype(SEND_Z)
        for d in (2, 1, 3):
            z_sum(j, d).start()

    def stage_b(j):
        total = part_own[chunk(j), tile_cols(0)]
        for d in (1, 3, 2):
            z_sum(j, d).wait_recv()
            total += zrecv[d - 1, chunk(j), :].astype(F32)
        pre[chunk(j), tile_cols(0, g * width + y * quarter)] = total.astype(BF16)
        for d in (2, 1, 3):
            z_gather(j, d).start()

    def stage_c(j):
        for d in (1, 3, 2):
            z_gather(j, d).wait_recv()
        x_gather(j, 0).start()
        y_gather(j).start()

    def stage_d(j):
        y_gather(j).wait_recv()
        x_gather(j, 1).start()

    def score(acc, who_c, who_g, who_y, first):
        some = pl.ds(pl.multiple_of(who_c * half_q, half_q), half_q)
        part = tile_scores(g_buf[:, share(who_g, who_y)], pre[some, share(who_g, who_y)])
        if first:
            acc[...] = part
        else:
            acc[...] += part

    n = CHUNKS // 2
    for s in range(CHUNKS + 3):
        if s >= 3:
            stage_d(s - 3)
        if 0 <= s - 2 < CHUNKS:
            stage_c(s - 2)
        if 0 <= s - 1 < CHUNKS:
            stage_b(s - 1)
        if s < CHUNKS:
            stage_a(s)
        if s == n + 1:
            for i in range(8):
                g_copy(i).wait()
            score(acc_far, 1 - c, g, y, True)
        if s == n + 2:
            score(acc_far, 1 - c, g, 1 - y, False)

    for which in range(2):
        for j in range(n):
            x_gather(j, which).wait_recv()
        score(acc_far, 1 - c, 1 - g, y if which == 0 else 1 - y, False)
    far = remote(acc_far, recv_sc, ss, sr, core)
    far.start()
    score(acc_own, c, g, y, True)
    score(acc_own, c, g, 1 - y, False)
    for which in range(2):
        for j in range(n, CHUNKS):
            x_gather(j, which).wait_recv()
        score(acc_own, c, 1 - g, y if which == 0 else 1 - y, False)
    far.wait_recv()
    out_ref[...] = acc_own[...] + recv_sc[...]

    t_send.wait_send()
    far.wait_send()
    for j in range(CHUNKS):
        y_sum(j).wait_send()
        y_gather(j).wait_send()
        for which in range(2):
            x_gather(j, which).wait_send()
        for d in range(1, NZ):
            z_sum(j, d).wait_send()
            z_gather(j, d).wait_send()


def fused(train_grads, test_grads, fisher_inverse):
    docs, half_k = train_grads.shape
    half_q, depth = test_grads.shape
    queries = 2 * half_q
    width = half_k // 2
    quarter = width // 2
    tile = quarter // NZ
    dma = pltpu.SemaphoreType.DMA
    scratch = [
        pltpu.VMEM((depth, width), F32),
        pltpu.VMEM((docs, half_k), BF16),
        pltpu.VMEM((queries, depth), F32),
        pltpu.VMEM((2 * queries, depth), BF16),
        pltpu.VMEM((queries, quarter), SEND_Y),
        pltpu.VMEM((queries, quarter), SEND_Y),
        pltpu.VMEM((queries, quarter), F32),
        pltpu.VMEM((queries, quarter), SEND_Z),
        pltpu.VMEM((NZ - 1, queries, tile), SEND_Z),
        pltpu.VMEM((queries, half_k), BF16),
        pltpu.VMEM((docs, half_q), F32),
        pltpu.VMEM((docs, half_q), F32),
        pltpu.VMEM((docs, half_q), F32),
        dma((2 * NZ,)), dma((8,)), dma, dma, dma,
        dma((CHUNKS,)), dma((CHUNKS,)),
        dma((CHUNKS, NZ - 1)), dma((CHUNKS, NZ - 1)),
        dma((CHUNKS, NZ - 1)), dma((CHUNKS, NZ - 1)),
        dma((CHUNKS,)), dma((CHUNKS,)),
        dma((CHUNKS, 2)), dma((CHUNKS, 2)),
        dma, dma,
    ]
    flops = 2 * queries * (3 * depth * width + docs * half_k)
    return pl.pallas_call(
        kernel,
        out_shape=jax.ShapeDtypeStruct((docs, half_q), F32),
        in_specs=[pl.BlockSpec(memory_space=pl.ANY)] * 3,
        out_specs=pl.BlockSpec(memory_space=pltpu.VMEM),
        scratch_shapes=scratch,
        compiler_params=pltpu.CompilerParams(
            collective_id=0, has_side_effects=True, vmem_limit_bytes=56 * 2**20
        ),
        cost_estimate=pl.CostEstimate(
            flops=flops, bytes_accessed=2 * docs * half_k + 4 * depth * width, transcendentals=0
        ),
    )(train_grads, test_grads, fisher_inverse)


def plain(train_grads, test_grads, fisher_inverse):
    queries = lax.all_gather(test_grads, "test", axis=0, tiled=True)
    share = lax.psum_scatter(
        jnp.dot(
            queries,
            fisher_inverse,
            precision=lax.Precision.HIGHEST,
            preferred_element_type=F32,
        ),
        "train",
        scatter_dimension=0,
        tiled=True,
    ).astype(BF16)
    preconditioned = lax.all_gather(share, "train", axis=0, tiled=True)
    partial_scores = tile_scores(train_grads, preconditioned)
    return lax.psum_scatter(partial_scores, "test", scatter_dimension=1, tiled=True)


def solution(mesh):
    sizes = (mesh.shape["groups"], mesh.shape["train"], mesh.shape["test"])
    body = fused if sizes == (2, NY * NZ, 2) else plain
    in_specs = (P(("groups", "train"), "test"), P("test", "train"), P("train", "test"))
    out_specs = P(("groups", "train"), "test")
    return jax.shard_map(
        body, mesh=mesh, in_specs=in_specs, out_specs=out_specs, check_vma=False
    )
```

```python
import jax
import jax.numpy as jnp
from jax import lax
from jax.experimental import pallas as pl
from jax.experimental.pallas import tpu as pltpu
from jax.sharding import PartitionSpec as P

MESH = pl.DeviceIdType.MESH
F32 = jnp.float32
BF16 = jnp.bfloat16

NY = 2
NZ = 4
LAG = 2
CHUNKS = 8
SEND_Y = BF16
SEND_Z = BF16


def tile_scores(train_grads, pieces):
    return lax.dot_general(
        train_grads, pieces, (((1,), (1,)), ((), ())), preferred_element_type=F32
    )


def kernel(
    train_ref, test_ref, fisher_ref, out_ref,
    f_buf, g_buf, t_buf, lhs, part_nb, recv_y, part_own, zsend, zrecv, pre,
    acc_far, acc_own, recv_sc,
    f_sem, g_sem, t_sem, ts_sem, tr_sem, ys, yr, zs, zr, gs, gr, cs, cr, xs, xr, ss, sr,
):
    queries, depth = t_buf.shape
    half_q = queries // 2
    width = f_buf.shape[1]
    quarter = width // 2
    tile = quarter // NZ
    rows = queries // CHUNKS
    pair = 2 * tile
    stride = quarter * NY

    g = lax.axis_index("groups")
    t = lax.axis_index("train")
    c = lax.axis_index("test")
    z = t // NY
    y = t % NY
    core = (g, t, 1 - c)
    side = (g, z * NY + 1 - y, c)
    twin = (1 - g, t, c)

    def peer(d):
        return (g, lax.rem(z + d, NZ) * NY + y, c)

    def column(who_g, who_y, piece):
        return piece * stride + who_y * quarter + who_g * pair

    def f_copy(i):
        who = jnp.where(i < NZ, 1 - y, y) if not isinstance(i, int) else (1 - y if i < NZ else y)
        k = i % NZ
        start = column(g, who, k // 2) + (k % 2) * tile
        return pltpu.make_async_copy(
            fisher_ref.at[:, pl.ds(pl.multiple_of(start, tile), tile)],
            f_buf.at[:, pl.ds(pl.multiple_of(i * tile, tile), tile)],
            f_sem.at[i],
        )

    def g_copy(i):
        who_g, who_y, piece = i // 4, (i // 2) % 2, i % 2
        return pltpu.make_async_copy(
            train_ref.at[:, pl.ds(column(who_g, who_y, piece), pair)],
            g_buf.at[:, pl.ds(i * pair, pair)],
            g_sem.at[i],
        )

    mine = pl.ds(pl.multiple_of(c * half_q, half_q), half_q)
    t_copy = pltpu.make_async_copy(test_ref, t_buf.at[mine], t_sem)
    t_copy.start()
    for i in range(2 * NZ):
        f_copy(i).start()

    barrier = pltpu.get_barrier_semaphore()
    friends = [core, side, twin] + [peer(d) for d in range(1, NZ)]
    for friend in friends:
        pl.semaphore_signal(barrier, inc=1, device_id=friend, device_id_type=MESH)
    pl.semaphore_wait(barrier, len(friends))

    def remote(src, dst, send, recv, where):
        return pltpu.make_async_remote_copy(
            src_ref=src, dst_ref=dst, send_sem=send, recv_sem=recv,
            device_id=where, device_id_type=MESH,
        )

    t_send = remote(test_ref, t_buf.at[mine], ts_sem, tr_sem, core)
    t_send.start()
    for i in range(8):
        g_copy(i).start()
    t_copy.wait()
    t_send.wait_recv()
    values = t_buf[...]
    high = values.astype(BF16)
    lhs[:queries, :] = high
    lhs[queries:, :] = (values - high.astype(F32)).astype(BF16)

    def product(i):
        f_copy(i).wait()
        f = f_buf[:, pl.ds(pl.multiple_of(i * tile, tile), tile)]
        f_high = f.astype(BF16)
        f_low = (f - f_high.astype(F32)).astype(BF16)
        both = jnp.dot(lhs[...], f_high, preferred_element_type=F32)
        cross = jnp.dot(lhs[:queries, :], f_low, preferred_element_type=F32)
        return both[:queries] + (both[queries:] + cross)

    @pl.loop(0, NZ)
    def _(i):
        part_nb[:, pl.ds(pl.multiple_of(i * tile, tile), tile)] = product(i).astype(SEND_Y)

    def chunk(j):
        n = CHUNKS // 2
        start = (1 - c) * half_q + j * rows if j < n else c * half_q + (j - n) * rows
        return pl.ds(pl.multiple_of(start, rows), rows)

    def y_sum(j):
        return remote(part_nb.at[chunk(j)], recv_y.at[chunk(j)], ys.at[j], yr.at[j], side)

    for j in range(CHUNKS):
        y_sum(j).start()

    @pl.loop(NZ, 2 * NZ)
    def _(i):
        part_own[:, pl.ds(pl.multiple_of((i - NZ) * tile, tile), tile)] = product(i)

    def tile_of(d):
        k = lax.rem(z + d + NZ - 2 * c, NZ)
        return (k % 2) * 2 + k // 2

    def tile_cols(d, base=0):
        return pl.ds(pl.multiple_of(base + tile_of(d) * tile, tile), tile)

    def share(who_g, who_y):
        start = who_g * width + who_y * quarter
        return pl.ds(pl.multiple_of(start, quarter), quarter)

    def z_sum(j, d):
        return remote(
            zsend.at[chunk(j), tile_cols(d)], zrecv.at[d - 1, chunk(j)],
            zs.at[j, d - 1], zr.at[j, d - 1], peer(d),
        )

    def z_gather(j, d):
        place = pre.at[chunk(j), tile_cols(0, g * width + y * quarter)]
        return remote(place, place, gs.at[j, d - 1], gr.at[j, d - 1], peer(d))

    def part_of(who_g, who_y, piece):
        start = who_g * width + who_y * quarter + piece * pair
        return pl.ds(pl.multiple_of(start, pair), pair)

    def y_gather(j, which):
        place = pre.at[chunk(j), share(g, y) if which == 0 else part_of(1 - g, y, 1)]
        return remote(place, place, cs.at[j, which], cr.at[j, which], side)

    def x_gather(j, which):
        place = pre.at[chunk(j), share(g, y) if which == 0 else part_of(g, 1 - y, 0)]
        return remote(place, place, xs.at[j, which], xr.at[j, which], twin)

    def stage_a(j):
        y_sum(j).wait_recv()
        total = part_own[chunk(j), :] + recv_y[chunk(j), :].astype(F32)
        part_own[chunk(j), :] = total
        zsend[chunk(j), :] = total.astype(SEND_Z)
        for d in (2, 1, 3):
            z_sum(j, d).start()

    def stage_b(j):
        total = part_own[chunk(j), tile_cols(0)]
        for d in (1, 3, 2):
            z_sum(j, d).wait_recv()
            total += zrecv[d - 1, chunk(j), :].astype(F32)
        pre[chunk(j), tile_cols(0, g * width + y * quarter)] = total.astype(BF16)
        for d in (2, 1, 3):
            z_gather(j, d).start()

    def stage_c(j):
        for d in (1, 3, 2):
            z_gather(j, d).wait_recv()
        x_gather(j, 0).start()
        y_gather(j, 0).start()

    def stage_d(j):
        y_gather(j, 0).wait_recv()
        x_gather(j, 1).start()
        x_gather(j, 0).wait_recv()
        y_gather(j, 1).start()

    def score(acc, who_c, who_g, who_y, first):
        some = pl.ds(pl.multiple_of(who_c * half_q, half_q), half_q)
        part = tile_scores(g_buf[:, share(who_g, who_y)], pre[some, share(who_g, who_y)])
        if first:
            acc[...] = part
        else:
            acc[...] += part

    n = CHUNKS // 2
    stages = (stage_a, stage_b, stage_c, stage_d)
    for s in range(CHUNKS + 3 * LAG):
        for k in (3, 2, 1, 0):
            if 0 <= s - k * LAG < CHUNKS:
                stages[k](s - k * LAG)
        if s == 0:
            for i in range(8):
                g_copy(i).wait()
        if s == n - 1 + 3 * LAG:
            score(acc_far, 1 - c, g, y, True)
        if s == n + 3 * LAG:
            score(acc_far, 1 - c, g, 1 - y, False)
        if s == n + 1 + 3 * LAG:
            score(acc_far, 1 - c, 1 - g, y, False)

    for j in range(n):
        x_gather(j, 1).wait_recv()
        y_gather(j, 1).wait_recv()
    score(acc_far, 1 - c, 1 - g, 1 - y, False)
    far = remote(acc_far, recv_sc, ss, sr, core)
    far.start()
    score(acc_own, c, g, y, True)
    score(acc_own, c, g, 1 - y, False)
    score(acc_own, c, 1 - g, y, False)
    for j in range(n, CHUNKS):
        x_gather(j, 1).wait_recv()
        y_gather(j, 1).wait_recv()
    score(acc_own, c, 1 - g, 1 - y, False)
    far.wait_recv()
    out_ref[...] = acc_own[...] + recv_sc[...]

    t_send.wait_send()
    far.wait_send()
    for j in range(CHUNKS):
        y_sum(j).wait_send()
        for which in range(2):
            x_gather(j, which).wait_send()
            y_gather(j, which).wait_send()
        for d in range(1, NZ):
            z_sum(j, d).wait_send()
            z_gather(j, d).wait_send()


def fused(train_grads, test_grads, fisher_inverse):
    docs, half_k = train_grads.shape
    half_q, depth = test_grads.shape
    queries = 2 * half_q
    width = half_k // 2
    quarter = width // 2
    tile = quarter // NZ
    dma = pltpu.SemaphoreType.DMA
    scratch = [
        pltpu.VMEM((depth, width), F32),
        pltpu.VMEM((docs, half_k), BF16),
        pltpu.VMEM((queries, depth), F32),
        pltpu.VMEM((2 * queries, depth), BF16),
        pltpu.VMEM((queries, quarter), SEND_Y),
        pltpu.VMEM((queries, quarter), SEND_Y),
        pltpu.VMEM((queries, quarter), F32),
        pltpu.VMEM((queries, quarter), SEND_Z),
        pltpu.VMEM((NZ - 1, queries, tile), SEND_Z),
        pltpu.VMEM((queries, half_k), BF16),
        pltpu.VMEM((docs, half_q), F32),
        pltpu.VMEM((docs, half_q), F32),
        pltpu.VMEM((docs, half_q), F32),
        dma((2 * NZ,)), dma((8,)), dma, dma, dma,
        dma((CHUNKS,)), dma((CHUNKS,)),
        dma((CHUNKS, NZ - 1)), dma((CHUNKS, NZ - 1)),
        dma((CHUNKS, NZ - 1)), dma((CHUNKS, NZ - 1)),
        dma((CHUNKS, 2)), dma((CHUNKS, 2)),
        dma((CHUNKS, 2)), dma((CHUNKS, 2)),
        dma, dma,
    ]
    flops = 2 * queries * (3 * depth * width + docs * half_k)
    return pl.pallas_call(
        kernel,
        out_shape=jax.ShapeDtypeStruct((docs, half_q), F32),
        in_specs=[pl.BlockSpec(memory_space=pl.ANY)] * 3,
        out_specs=pl.BlockSpec(memory_space=pltpu.VMEM),
        scratch_shapes=scratch,
        compiler_params=pltpu.CompilerParams(
            collective_id=0, has_side_effects=True, vmem_limit_bytes=56 * 2**20
        ),
        cost_estimate=pl.CostEstimate(
            flops=flops, bytes_accessed=2 * docs * half_k + 4 * depth * width, transcendentals=0
        ),
    )(train_grads, test_grads, fisher_inverse)


def plain(train_grads, test_grads, fisher_inverse):
    queries = lax.all_gather(test_grads, "test", axis=0, tiled=True)
    share = lax.psum_scatter(
        jnp.dot(
            queries,
            fisher_inverse,
            precision=lax.Precision.HIGHEST,
            preferred_element_type=F32,
        ),
        "train",
        scatter_dimension=0,
        tiled=True,
    ).astype(BF16)
    preconditioned = lax.all_gather(share, "train", axis=0, tiled=True)
    partial_scores = tile_scores(train_grads, preconditioned)
    return lax.psum_scatter(partial_scores, "test", scatter_dimension=1, tiled=True)


def solution(mesh):
    sizes = (mesh.shape["groups"], mesh.shape["train"], mesh.shape["test"])
    body = fused if sizes == (2, NY * NZ, 2) else plain
    in_specs = (P(("groups", "train"), "test"), P("test", "train"), P("train", "test"))
    out_specs = P(("groups", "train"), "test")
    return jax.shard_map(
        body, mesh=mesh, in_specs=in_specs, out_specs=out_specs, check_vma=False
    )
```

```python
import jax
import jax.numpy as jnp
from jax import lax
from jax.experimental import pallas as pl
from jax.experimental.pallas import tpu as pltpu
from jax.sharding import PartitionSpec as P

MESH = pl.DeviceIdType.MESH
F32 = jnp.float32
BF16 = jnp.bfloat16

NY = 2
NZ = 4
DIRECT = (7,)
STEPS_DIRECT = (0, 3, 6, 9)
STEPS_FORWARD = (0, 3, 5, 7, 9)
CHUNKS = 8
SEND_Y = BF16
SEND_Z = BF16


def tile_scores(train_grads, pieces):
    return lax.dot_general(
        train_grads, pieces, (((1,), (1,)), ((), ())), preferred_element_type=F32
    )


def kernel(
    train_ref, test_ref, fisher_ref, acc_own, recv_sc,
    f_buf, g_buf, t_buf, lhs, part_nb, recv_y, part_own, dsend, drecv, pre,
    acc_far,
    f_sem, g_sem, t_sem, ts_sem, tr_sem, ys, yr, ds, dr, es, er, cs, cr, xs, xr,
    ss, sr,
):
    queries, depth = t_buf.shape
    half_q = queries // 2
    width = f_buf.shape[1]
    quarter = width // 2
    tile = quarter // NZ
    rows = queries // CHUNKS
    pair = 2 * tile
    stride = quarter * NY

    g = lax.axis_index("groups")
    t = lax.axis_index("train")
    c = lax.axis_index("test")
    z = t // NY
    y = t % NY
    core = (g, t, 1 - c)
    side = (g, z * NY + 1 - y, c)
    twin = (1 - g, t, c)

    def peer(d):
        return (g, lax.rem(z + d, NZ) * NY + y, c)

    e = z % 2
    buddy = (g, (z + 1 - 2 * e) * NY + y, c)
    across = (g, lax.rem(z + 2, NZ) * NY + y, c)
    third = (g, lax.rem(z + 3 - 2 * e, NZ) * NY + y, c)

    def column(who_g, who_y, piece):
        return piece * stride + who_y * quarter + who_g * pair

    def f_copy(i):
        who = jnp.where(i < NZ, 1 - y, y) if not isinstance(i, int) else (1 - y if i < NZ else y)
        k = i % NZ
        start = column(g, who, k // 2) + (k % 2) * tile
        return pltpu.make_async_copy(
            fisher_ref.at[:, pl.ds(pl.multiple_of(start, tile), tile)],
            f_buf.at[:, pl.ds(pl.multiple_of(i * tile, tile), tile)],
            f_sem.at[i],
        )

    def g_copy(i):
        who_g, who_y, piece = i // 4, (i // 2) % 2, i % 2
        return pltpu.make_async_copy(
            train_ref.at[:, pl.ds(column(who_g, who_y, piece), pair)],
            g_buf.at[:, pl.ds(i * pair, pair)],
            g_sem.at[i],
        )

    mine = pl.ds(pl.multiple_of(c * half_q, half_q), half_q)
    t_copy = pltpu.make_async_copy(test_ref, t_buf.at[mine], t_sem)
    t_copy.start()
    for i in range(NZ):
        f_copy(i).start()

    barrier = pltpu.get_barrier_semaphore()
    friends = [core, side, twin] + [peer(d) for d in range(1, NZ)]
    for friend in friends:
        pl.semaphore_signal(barrier, inc=1, device_id=friend, device_id_type=MESH)

    def remote(src, dst, send, recv, where):
        return pltpu.make_async_remote_copy(
            src_ref=src, dst_ref=dst, send_sem=send, recv_sem=recv,
            device_id=where, device_id_type=MESH,
        )

    pl.semaphore_wait(barrier, len(friends))
    t_send = remote(test_ref, t_buf.at[mine], ts_sem, tr_sem, core)
    t_send.start()

    def split(some, low):
        values = t_buf[some, :]
        high = values.astype(BF16)
        lhs[some, :] = high
        lhs[low, :] = (values - high.astype(F32)).astype(BF16)

    def product(i, some, low):
        f = f_buf[:, pl.ds(pl.multiple_of(i * tile, tile), tile)]
        f_high = f.astype(BF16)
        f_low = (f - f_high.astype(F32)).astype(BF16)
        small = jnp.dot(lhs[low, :], f_high, preferred_element_type=F32)
        small += jnp.dot(lhs[some, :], f_low, preferred_element_type=F32)
        return small + jnp.dot(lhs[some, :], f_high, preferred_element_type=F32)

    def half(who):
        some = pl.ds(pl.multiple_of(who * half_q, half_q), half_q)
        return some, pl.ds(pl.multiple_of(queries + who * half_q, half_q), half_q)

    def chunk(j):
        n = CHUNKS // 4
        if j < n:
            start = c * half_q + j * rows
        elif j < 3 * n:
            start = (1 - c) * half_q + (j - n) * rows
        else:
            start = c * half_q + (j - 2 * n) * rows
        return pl.ds(pl.multiple_of(start, rows), rows)

    def y_sum(j):
        return remote(part_nb.at[chunk(j)], recv_y.at[chunk(j)], ys.at[j], yr.at[j], side)

    t_copy.wait()
    split(*half(c))

    @pl.loop(0, NZ)
    def _(i):
        f_copy(i).wait()
        some, low = half(c)
        cols = pl.ds(pl.multiple_of(i * tile, tile), tile)
        part_nb[some, cols] = product(i, some, low).astype(SEND_Y)

    for j in range(CHUNKS // 4):
        y_sum(j).start()
    for i in range(NZ, 2 * NZ):
        f_copy(i).start()
    t_send.wait_recv()
    split(*half(1 - c))

    @pl.loop(0, NZ)
    def _(i):
        some, low = half(1 - c)
        cols = pl.ds(pl.multiple_of(i * tile, tile), tile)
        part_nb[some, cols] = product(i, some, low).astype(SEND_Y)

    for j in range(CHUNKS // 4, CHUNKS):
        y_sum(j).start()
    for i in range(8):
        g_copy(i).start()

    @pl.loop(NZ, 2 * NZ)
    def _(i):
        f_copy(i).wait()
        cols = pl.ds(pl.multiple_of((i - NZ) * tile, tile), tile)
        part_own[:, cols] = product(i, pl.ds(0, queries), pl.ds(queries, queries))

    def share(who_g, who_y):
        start = who_g * width + who_y * quarter
        return pl.ds(pl.multiple_of(start, quarter), quarter)

    here = g * width + y * quarter

    def tile_at(d, base=0):
        k = lax.rem(z + d + NZ - 2 * c, NZ)
        return pl.ds(pl.multiple_of(base + ((k % 2) * 2 + k // 2) * tile, tile), tile)

    def d_sum(j, d):
        return remote(
            dsend.at[chunk(j), tile_at(d)], drecv.at[d - 1, chunk(j)],
            ds.at[j, d - 1], dr.at[j, d - 1], peer(d),
        )

    def d_gather(j, role):
        place = pre.at[chunk(j), tile_at(0, here)]
        return remote(
            place, place, es.at[j, role], er.at[j, role], (buddy, across, third)[role]
        )

    def forward(j):
        place = pre.at[chunk(j), tile_at(2, here)]
        return remote(place, place, es.at[j, 2], er.at[j, 2], buddy)

    def part_of(who_g, who_y, piece):
        start = who_g * width + who_y * quarter + piece * pair
        return pl.ds(pl.multiple_of(start, pair), pair)

    def y_gather(j, which):
        place = pre.at[chunk(j), share(g, y) if which == 0 else part_of(1 - g, y, 1)]
        return remote(place, place, cs.at[j, which], cr.at[j, which], side)

    def x_gather(j, which):
        place = pre.at[chunk(j), share(g, y) if which == 0 else part_of(g, 1 - y, 0)]
        return remote(place, place, xs.at[j, which], xr.at[j, which], twin)

    def sum_y(j):
        y_sum(j).wait_recv()
        some = chunk(j)
        total = part_own[some, :] + recv_y[some, :].astype(F32)
        part_own[some, :] = total
        dsend[some, :] = total.astype(SEND_Z)
        for d in (2, 1, 3):
            d_sum(j, d).start()

    def sum_z(j):
        some = chunk(j)
        total = part_own[some, tile_at(0)]
        for d in (1, 3, 2):
            d_sum(j, d).wait_recv()
            total += drecv[d - 1, some, :].astype(F32)
        pre[some, tile_at(0, here)] = total.astype(BF16)
        d_gather(j, 1).start()
        if j in DIRECT:
            d_gather(j, 2).start()
        d_gather(j, 0).start()

    def pass_on(j):
        d_gather(j, 1).wait_recv()
        forward(j).start()

    def gather_sides(j):
        d_gather(j, 0).wait_recv()
        if j in DIRECT:
            d_gather(j, 1).wait_recv()
        d_gather(j, 2).wait_recv()
        x_gather(j, 0).start()
        y_gather(j, 0).start()

    def gather_rest(j):
        y_gather(j, 0).wait_recv()
        x_gather(j, 1).start()
        x_gather(j, 0).wait_recv()
        y_gather(j, 1).start()

    def score(acc, who_c, who_g, who_y, first):
        some = pl.ds(pl.multiple_of(who_c * half_q, half_q), half_q)
        part = tile_scores(g_buf[:, share(who_g, who_y)], pre[some, share(who_g, who_y)])
        if first:
            acc[...] = part
        else:
            acc[...] += part

    n = CHUNKS // 4
    direct = list(zip(STEPS_DIRECT, (sum_y, sum_z, gather_sides, gather_rest)))
    pairs = list(zip(STEPS_FORWARD, (sum_y, sum_z, pass_on, gather_sides, gather_rest)))
    plan = []
    for j in range(CHUNKS):
        for k, (step, stage) in enumerate(direct if j in DIRECT else pairs):
            plan.append((j + step, j, k, stage))
    plan.sort(key=lambda p: p[:3])
    far_rows, own_rows = set(range(n, 3 * n)), set(range(CHUNKS)) - set(range(n, 3 * n))

    sides, rests = set(), set()
    for _, j, _, stage in plan:
        stage(j)
        if stage is gather_sides:
            sides.add(j)
        if stage is gather_rest:
            rests.add(j)
        if stage is gather_sides and sides >= far_rows and j in far_rows:
            for i in range(8):
                g_copy(i).wait()
            score(acc_far, 1 - c, g, y, True)
        if stage is gather_rest and rests >= far_rows and j in far_rows:
            score(acc_far, 1 - c, g, 1 - y, False)
            score(acc_far, 1 - c, 1 - g, y, False)
        if stage is gather_sides and len(sides) == CHUNKS:
            score(acc_own, c, g, y, True)

    for j in sorted(far_rows):
        x_gather(j, 1).wait_recv()
        y_gather(j, 1).wait_recv()
    score(acc_far, 1 - c, 1 - g, 1 - y, False)
    far = remote(acc_far, recv_sc, ss, sr, core)
    far.start()
    score(acc_own, c, g, 1 - y, False)
    score(acc_own, c, 1 - g, y, False)
    for j in sorted(own_rows):
        x_gather(j, 1).wait_recv()
        y_gather(j, 1).wait_recv()
    score(acc_own, c, 1 - g, 1 - y, False)
    far.wait_recv()

    t_send.wait_send()
    far.wait_send()
    for j in range(CHUNKS):
        y_sum(j).wait_send()
        for which in range(2):
            x_gather(j, which).wait_send()
            y_gather(j, which).wait_send()
        for d in range(1, NZ):
            d_sum(j, d).wait_send()
        d_gather(j, 0).wait_send()
        d_gather(j, 1).wait_send()
        (d_gather(j, 2) if j in DIRECT else forward(j)).wait_send()


def fused(train_grads, test_grads, fisher_inverse):
    docs, half_k = train_grads.shape
    half_q, depth = test_grads.shape
    queries = 2 * half_q
    width = half_k // 2
    quarter = width // 2
    tile = quarter // NZ
    dma = pltpu.SemaphoreType.DMA
    scratch = [
        pltpu.VMEM((depth, width), F32),
        pltpu.VMEM((docs, half_k), BF16),
        pltpu.VMEM((queries, depth), F32),
        pltpu.VMEM((2 * queries, depth), BF16),
        pltpu.VMEM((queries, quarter), SEND_Y),
        pltpu.VMEM((queries, quarter), SEND_Y),
        pltpu.VMEM((queries, quarter), F32),
        pltpu.VMEM((queries, quarter), SEND_Z),
        pltpu.VMEM((NZ - 1, queries, tile), SEND_Z),
        pltpu.VMEM((queries, half_k), BF16),
        pltpu.VMEM((docs, half_q), F32),
        dma((2 * NZ,)), dma((8,)), dma, dma, dma,
        dma((CHUNKS,)), dma((CHUNKS,)),
        dma((CHUNKS, NZ - 1)), dma((CHUNKS, NZ - 1)), dma((CHUNKS, NZ - 1)), dma((CHUNKS, NZ - 1)),
        dma((CHUNKS, 2)), dma((CHUNKS, 2)),
        dma((CHUNKS, 2)), dma((CHUNKS, 2)),
        dma, dma,
    ]
    flops = 2 * queries * (3 * depth * width + docs * half_k)
    shape = jax.ShapeDtypeStruct((docs, half_q), F32)
    own, received = pl.pallas_call(
        kernel,
        out_shape=(shape, shape),
        in_specs=[pl.BlockSpec(memory_space=pl.ANY)] * 3,
        out_specs=[pl.BlockSpec(memory_space=pltpu.VMEM)] * 2,
        scratch_shapes=scratch,
        compiler_params=pltpu.CompilerParams(
            collective_id=0, has_side_effects=True, vmem_limit_bytes=56 * 2**20
        ),
        cost_estimate=pl.CostEstimate(
            flops=flops, bytes_accessed=2 * docs * half_k + 4 * depth * width, transcendentals=0
        ),
    )(train_grads, test_grads, fisher_inverse)
    return own + received


def plain(train_grads, test_grads, fisher_inverse):
    queries = lax.all_gather(test_grads, "test", axis=0, tiled=True)
    share = lax.psum_scatter(
        jnp.dot(
            queries,
            fisher_inverse,
            precision=lax.Precision.HIGHEST,
            preferred_element_type=F32,
        ),
        "train",
        scatter_dimension=0,
        tiled=True,
    ).astype(BF16)
    preconditioned = lax.all_gather(share, "train", axis=0, tiled=True)
    partial_scores = tile_scores(train_grads, preconditioned)
    return lax.psum_scatter(partial_scores, "test", scatter_dimension=1, tiled=True)


def solution(mesh):
    sizes = (mesh.shape["groups"], mesh.shape["train"], mesh.shape["test"])
    body = fused if sizes == (2, NY * NZ, 2) else plain
    in_specs = (P(("groups", "train"), "test"), P("test", "train"), P("train", "test"))
    out_specs = P(("groups", "train"), "test")
    return jax.shard_map(
        body, mesh=mesh, in_specs=in_specs, out_specs=out_specs, check_vma=False
    )
```

```python
import jax
import jax.numpy as jnp
from jax import lax
from jax.experimental import pallas as pl
from jax.experimental.pallas import tpu as pltpu
from jax.sharding import PartitionSpec as P

MESH = pl.DeviceIdType.MESH
F32 = jnp.float32
BF16 = jnp.bfloat16

NY = 2
NZ = 4
DIRECT = (6, 7)
STEPS_DIRECT = (0, 3, 6, 8)
STEPS_FORWARD = (0, 3, 5, 7, 9)
CHUNKS = 8
SEND_Y = BF16
SEND_Z = BF16


def tile_scores(train_grads, pieces):
    return lax.dot_general(
        train_grads, pieces, (((1,), (1,)), ((), ())), preferred_element_type=F32
    )


def kernel(
    train_ref, test_ref, fisher_ref, acc_own, recv_sc,
    f_buf, g_buf, t_buf, lhs, part_nb, recv_y, part_own, dsend, drecv, pre,
    acc_far,
    f_sem, g_sem, t_sem, ts_sem, tr_sem, ys, yr, ds, dr, es, er, cs, cr, xs, xr,
    ss, sr,
):
    queries, depth = t_buf.shape
    half_q = queries // 2
    width = f_buf.shape[1]
    quarter = width // 2
    tile = quarter // NZ
    rows = queries // CHUNKS
    pair = 2 * tile
    stride = quarter * NY

    g = lax.axis_index("groups")
    t = lax.axis_index("train")
    c = lax.axis_index("test")
    z = t // NY
    y = t % NY
    core = (g, t, 1 - c)
    side = (g, z * NY + 1 - y, c)
    twin = (1 - g, t, c)

    def peer(d):
        return (g, lax.rem(z + d, NZ) * NY + y, c)

    e = z % 2
    buddy = (g, (z + 1 - 2 * e) * NY + y, c)
    across = (g, lax.rem(z + 2, NZ) * NY + y, c)
    third = (g, lax.rem(z + 3 - 2 * e, NZ) * NY + y, c)

    def column(who_g, who_y, piece):
        return piece * stride + who_y * quarter + who_g * pair

    def f_copy(i):
        who = jnp.where(i < NZ, 1 - y, y) if not isinstance(i, int) else (1 - y if i < NZ else y)
        k = i % NZ
        start = column(g, who, k // 2) + (k % 2) * tile
        return pltpu.make_async_copy(
            fisher_ref.at[:, pl.ds(pl.multiple_of(start, tile), tile)],
            f_buf.at[:, pl.ds(pl.multiple_of(i * tile, tile), tile)],
            f_sem.at[i],
        )

    def g_copy(i):
        who_g, who_y, piece = i // 4, (i // 2) % 2, i % 2
        return pltpu.make_async_copy(
            train_ref.at[:, pl.ds(column(who_g, who_y, piece), pair)],
            g_buf.at[:, pl.ds(i * pair, pair)],
            g_sem.at[i],
        )

    mine = pl.ds(pl.multiple_of(c * half_q, half_q), half_q)
    t_copy = pltpu.make_async_copy(test_ref, t_buf.at[mine], t_sem)
    t_copy.start()
    for i in range(NZ):
        f_copy(i).start()

    barrier = pltpu.get_barrier_semaphore()
    friends = [core, side, twin] + [peer(d) for d in range(1, NZ)]
    for friend in friends:
        pl.semaphore_signal(barrier, inc=1, device_id=friend, device_id_type=MESH)

    def remote(src, dst, send, recv, where):
        return pltpu.make_async_remote_copy(
            src_ref=src, dst_ref=dst, send_sem=send, recv_sem=recv,
            device_id=where, device_id_type=MESH,
        )

    pl.semaphore_wait(barrier, len(friends))
    t_send = remote(test_ref, t_buf.at[mine], ts_sem, tr_sem, core)
    t_send.start()

    def split(some, low):
        values = t_buf[some, :]
        high = values.astype(BF16)
        lhs[some, :] = high
        lhs[low, :] = (values - high.astype(F32)).astype(BF16)

    def product(i, some, low):
        f = f_buf[:, pl.ds(pl.multiple_of(i * tile, tile), tile)]
        f_high = f.astype(BF16)
        f_low = (f - f_high.astype(F32)).astype(BF16)
        small = jnp.dot(lhs[low, :], f_high, preferred_element_type=F32)
        small += jnp.dot(lhs[some, :], f_low, preferred_element_type=F32)
        return small + jnp.dot(lhs[some, :], f_high, preferred_element_type=F32)

    def half(who):
        some = pl.ds(pl.multiple_of(who * half_q, half_q), half_q)
        return some, pl.ds(pl.multiple_of(queries + who * half_q, half_q), half_q)

    def chunk(j):
        n = CHUNKS // 4
        if j < n:
            start = c * half_q + j * rows
        elif j < 3 * n:
            start = (1 - c) * half_q + (j - n) * rows
        else:
            start = c * half_q + (j - 2 * n) * rows
        return pl.ds(pl.multiple_of(start, rows), rows)

    def y_sum(j):
        return remote(part_nb.at[chunk(j)], recv_y.at[chunk(j)], ys.at[j], yr.at[j], side)

    t_copy.wait()
    split(*half(c))

    @pl.loop(0, NZ)
    def _(i):
        f_copy(i).wait()
        some, low = half(c)
        cols = pl.ds(pl.multiple_of(i * tile, tile), tile)
        part_nb[some, cols] = product(i, some, low).astype(SEND_Y)

    for j in range(CHUNKS // 4):
        y_sum(j).start()
    for i in range(NZ, 2 * NZ):
        f_copy(i).start()
    t_send.wait_recv()
    split(*half(1 - c))

    @pl.loop(0, NZ)
    def _(i):
        some, low = half(1 - c)
        cols = pl.ds(pl.multiple_of(i * tile, tile), tile)
        part_nb[some, cols] = product(i, some, low).astype(SEND_Y)

    for j in range(CHUNKS // 4, CHUNKS):
        y_sum(j).start()
    for i in range(8):
        g_copy(i).start()

    @pl.loop(NZ, 2 * NZ)
    def _(i):
        f_copy(i).wait()
        cols = pl.ds(pl.multiple_of((i - NZ) * tile, tile), tile)
        part_own[:, cols] = product(i, pl.ds(0, queries), pl.ds(queries, queries))

    def share(who_g, who_y):
        start = who_g * width + who_y * quarter
        return pl.ds(pl.multiple_of(start, quarter), quarter)

    here = g * width + y * quarter

    def tile_at(d, base=0):
        k = lax.rem(z + d + NZ - 2 * c, NZ)
        return pl.ds(pl.multiple_of(base + ((k % 2) * 2 + k // 2) * tile, tile), tile)

    def d_sum(j, d):
        return remote(
            dsend.at[chunk(j), tile_at(d)], drecv.at[d - 1, chunk(j)],
            ds.at[j, d - 1], dr.at[j, d - 1], peer(d),
        )

    def d_gather(j, role):
        place = pre.at[chunk(j), tile_at(0, here)]
        return remote(
            place, place, es.at[j, role], er.at[j, role], (buddy, across, third)[role]
        )

    def forward(j):
        place = pre.at[chunk(j), tile_at(2, here)]
        return remote(place, place, es.at[j, 2], er.at[j, 2], buddy)

    def part_of(who_g, who_y, piece):
        start = who_g * width + who_y * quarter + piece * pair
        return pl.ds(pl.multiple_of(start, pair), pair)

    def y_gather(j, which):
        place = pre.at[chunk(j), share(g, y) if which == 0 else part_of(1 - g, y, 1)]
        return remote(place, place, cs.at[j, which], cr.at[j, which], side)

    def x_gather(j, which):
        place = pre.at[chunk(j), share(g, y) if which == 0 else part_of(g, 1 - y, 0)]
        return remote(place, place, xs.at[j, which], xr.at[j, which], twin)

    def sum_y(j):
        y_sum(j).wait_recv()
        some = chunk(j)
        total = part_own[some, :] + recv_y[some, :].astype(F32)
        part_own[some, :] = total
        dsend[some, :] = total.astype(SEND_Z)
        for d in (2, 1, 3):
            d_sum(j, d).start()

    def sum_z(j):
        some = chunk(j)
        total = part_own[some, tile_at(0)]
        for d in (1, 3, 2):
            d_sum(j, d).wait_recv()
            total += drecv[d - 1, some, :].astype(F32)
        pre[some, tile_at(0, here)] = total.astype(BF16)
        d_gather(j, 1).start()
        if j in DIRECT:
            d_gather(j, 2).start()
        d_gather(j, 0).start()

    def pass_on(j):
        d_gather(j, 1).wait_recv()
        forward(j).start()

    def gather_sides(j):
        d_gather(j, 0).wait_recv()
        if j in DIRECT:
            d_gather(j, 1).wait_recv()
        d_gather(j, 2).wait_recv()
        y_gather(j, 0).start()
        x_gather(j, 0).start()

    def gather_rest(j):
        y_gather(j, 0).wait_recv()
        x_gather(j, 1).start()
        x_gather(j, 0).wait_recv()
        y_gather(j, 1).start()

    def score(acc, who_c, who_g, who_y, first):
        some = pl.ds(pl.multiple_of(who_c * half_q, half_q), half_q)
        part = tile_scores(g_buf[:, share(who_g, who_y)], pre[some, share(who_g, who_y)])
        if first:
            acc[...] = part
        else:
            acc[...] += part

    n = CHUNKS // 4
    direct = list(zip(STEPS_DIRECT, (sum_y, sum_z, gather_sides, gather_rest)))
    pairs = list(zip(STEPS_FORWARD, (sum_y, sum_z, pass_on, gather_sides, gather_rest)))
    plan = []
    for j in range(CHUNKS):
        for k, (step, stage) in enumerate(direct if j in DIRECT else pairs):
            plan.append((j + step, j, k, stage))
    plan.sort(key=lambda p: p[:3])
    far_rows, own_rows = set(range(n, 3 * n)), set(range(CHUNKS)) - set(range(n, 3 * n))

    sides, rests = set(), set()
    for _, j, _, stage in plan:
        stage(j)
        if stage is gather_sides:
            sides.add(j)
        if stage is gather_rest:
            rests.add(j)
        if stage is gather_sides and sides >= far_rows and j in far_rows:
            for i in range(8):
                g_copy(i).wait()
            score(acc_far, 1 - c, g, y, True)
        if stage is gather_rest and rests >= far_rows and j in far_rows:
            score(acc_far, 1 - c, g, 1 - y, False)
            score(acc_far, 1 - c, 1 - g, y, False)
        if stage is gather_sides and len(sides) == CHUNKS:
            score(acc_own, c, g, y, True)

    for j in sorted(far_rows):
        x_gather(j, 1).wait_recv()
        y_gather(j, 1).wait_recv()
    score(acc_far, 1 - c, 1 - g, 1 - y, False)
    far = remote(acc_far, recv_sc, ss, sr, core)
    far.start()
    score(acc_own, c, g, 1 - y, False)
    score(acc_own, c, 1 - g, y, False)
    own = pl.ds(pl.multiple_of(c * half_q, half_q), half_q)
    for piece, gather in enumerate((x_gather, y_gather)):
        for j in sorted(own_rows):
            gather(j, 1).wait_recv()
        cols = part_of(1 - g, 1 - y, piece)
        acc_own[...] += tile_scores(g_buf[:, cols], pre[own, cols])
    far.wait_recv()

    t_send.wait_send()
    far.wait_send()
    for j in range(CHUNKS):
        y_sum(j).wait_send()
        for which in range(2):
            x_gather(j, which).wait_send()
            y_gather(j, which).wait_send()
        for d in range(1, NZ):
            d_sum(j, d).wait_send()
        d_gather(j, 0).wait_send()
        d_gather(j, 1).wait_send()
        (d_gather(j, 2) if j in DIRECT else forward(j)).wait_send()


def fused(train_grads, test_grads, fisher_inverse):
    docs, half_k = train_grads.shape
    half_q, depth = test_grads.shape
    queries = 2 * half_q
    width = half_k // 2
    quarter = width // 2
    tile = quarter // NZ
    dma = pltpu.SemaphoreType.DMA
    scratch = [
        pltpu.VMEM((depth, width), F32),
        pltpu.VMEM((docs, half_k), BF16),
        pltpu.VMEM((queries, depth), F32),
        pltpu.VMEM((2 * queries, depth), BF16),
        pltpu.VMEM((queries, quarter), SEND_Y),
        pltpu.VMEM((queries, quarter), SEND_Y),
        pltpu.VMEM((queries, quarter), F32),
        pltpu.VMEM((queries, quarter), SEND_Z),
        pltpu.VMEM((NZ - 1, queries, tile), SEND_Z),
        pltpu.VMEM((queries, half_k), BF16),
        pltpu.VMEM((docs, half_q), F32),
        dma((2 * NZ,)), dma((8,)), dma, dma, dma,
        dma((CHUNKS,)), dma((CHUNKS,)),
        dma((CHUNKS, NZ - 1)), dma((CHUNKS, NZ - 1)), dma((CHUNKS, NZ - 1)), dma((CHUNKS, NZ - 1)),
        dma((CHUNKS, 2)), dma((CHUNKS, 2)),
        dma((CHUNKS, 2)), dma((CHUNKS, 2)),
        dma, dma,
    ]
    flops = 2 * queries * (3 * depth * width + docs * half_k)
    shape = jax.ShapeDtypeStruct((docs, half_q), F32)
    own, received = pl.pallas_call(
        kernel,
        out_shape=(shape, shape),
        in_specs=[pl.BlockSpec(memory_space=pl.ANY)] * 3,
        out_specs=[pl.BlockSpec(memory_space=pltpu.VMEM)] * 2,
        scratch_shapes=scratch,
        compiler_params=pltpu.CompilerParams(
            collective_id=0, has_side_effects=True, vmem_limit_bytes=56 * 2**20
        ),
        cost_estimate=pl.CostEstimate(
            flops=flops, bytes_accessed=2 * docs * half_k + 4 * depth * width, transcendentals=0
        ),
    )(train_grads, test_grads, fisher_inverse)
    return own + received


def plain(train_grads, test_grads, fisher_inverse):
    queries = lax.all_gather(test_grads, "test", axis=0, tiled=True)
    share = lax.psum_scatter(
        jnp.dot(
            queries,
            fisher_inverse,
            precision=lax.Precision.HIGHEST,
            preferred_element_type=F32,
        ),
        "train",
        scatter_dimension=0,
        tiled=True,
    ).astype(BF16)
    preconditioned = lax.all_gather(share, "train", axis=0, tiled=True)
    partial_scores = tile_scores(train_grads, preconditioned)
    return lax.psum_scatter(partial_scores, "test", scatter_dimension=1, tiled=True)


def solution(mesh):
    sizes = (mesh.shape["groups"], mesh.shape["train"], mesh.shape["test"])
    body = fused if sizes == (2, NY * NZ, 2) else plain
    in_specs = (P(("groups", "train"), "test"), P("test", "train"), P("train", "test"))
    out_specs = P(("groups", "train"), "test")
    return jax.shard_map(
        body, mesh=mesh, in_specs=in_specs, out_specs=out_specs, check_vma=False
    )
```
